256 devices in a mesh: section: 16 (over z, core), dp: 8 (over y_lo, x), tensor: 2 (over y_hi).
Axes of the slice: x: 4, y: 4 (y_hi: 2, y_lo: 2; y = y_hi * 2 + y_lo), z: 8, core: 2. Of those that a mesh axis runs over, the one named last changes fastest.
Arguments:
- embeddings: bfloat16 [2048, 6144], P('dp', 'tensor'), may hold values from -110 to 110
- section_outputs: bfloat16 [16, 2048, 6144], P('section', 'dp', 'tensor'), may hold values from -110 to 110
- norm_gain: float32 [16, 6144], P('section', 'tensor'), may hold values from 0.1 to 1.9
- input_grads: bfloat16 [16, 2048, 6144], P('section', 'dp', 'tensor'), may hold values from -16 to 16
- loss_grads: bfloat16 [2048, 6144], P('dp', 'tensor'), may hold values from -16 to 16
Outputs:
- inverses: float32 [16, 2, 8, 768, 768], P('section', 'tensor', 'dp')
The draws below stay inside these ranges and needn't reach their ends.
All inputs are finite; a program needn't handle non-finite values. Where the reference program divides by a largest or mean magnitude, that divisor is 1e-20 or more.
Results may differ from the reference program's by a relative error of at most 0.0003.
Values may be sent and summed in bfloat16 or wider, within the bound.
No kernel may reach another device: no remote copies, remote signals or barrier semaphores. Data moves between devices by JAX's collectives and lax.ppermute only.
A program may use at most 128 MiB of HBM per device.

```python
import math
import jax
import jax.numpy as jnp
from jax import lax

D = 6144
BLK = 768
ITERS = 3
SECTIONS = 16
TOKENS = 2048


def stream_values(key, leading):
    subkeys = jax.random.split(key, 4)
    feature_scale = jnp.exp(jax.random.uniform(subkeys[0], (leading, 1, D), jnp.float32, math.log(0.3), math.log(3.0)))
    position = jnp.arange(D, dtype=jnp.float32) / D
    trend_scale = jnp.exp((position - 0.5) * math.log(3.0))
    row_scale = jnp.exp(jax.random.uniform(subkeys[1], (leading, TOKENS, 1), jnp.float32, math.log(0.5), math.log(5.0)))
    row_offset = jax.random.uniform(subkeys[2], (leading, TOKENS, 1), jnp.float32, -1.0, 1.0)
    fluctuation = jnp.clip(jax.random.normal(subkeys[3], (leading, TOKENS, D), jnp.float32), -4.0, 4.0)
    return (fluctuation * feature_scale * trend_scale + row_offset) * row_scale


def grad_values(key, leading):
    subkeys = jax.random.split(key, 3)
    feature_scale = jnp.exp(jax.random.uniform(subkeys[0], (leading, 1, D), jnp.float32, math.log(0.2), math.log(2.0)))
    row_scale = jnp.exp(jax.random.uniform(subkeys[1], (leading, TOKENS, 1), jnp.float32, math.log(0.5), math.log(2.0)))
    fluctuation = jnp.clip(jax.random.normal(subkeys[2], (leading, TOKENS, D), jnp.float32), -4.0, 4.0)
    return fluctuation * feature_scale * row_scale


def draw_embeddings(key, part):
    key = jax.random.fold_in(key, 13)
    return stream_values(key, 1)[0].astype(jnp.bfloat16)


def draw_section_outputs(key, part):
    key = jax.random.fold_in(key, 11)
    return stream_values(key, SECTIONS).astype(jnp.bfloat16)


def draw_input_grads(key, part):
    key = jax.random.fold_in(key, 12)
    return grad_values(key, SECTIONS).astype(jnp.bfloat16)


def draw_loss_grads(key, part):
    key = jax.random.fold_in(key, 14)
    return grad_values(key, 1)[0].astype(jnp.bfloat16)


def setup_inputs(seed: int = 0) -> dict:
    key_of = jax.random.split(jax.random.key(seed), 6)
    embeddings = draw_embeddings(jax.random.fold_in(key_of[5], 71), 0)
    section_outputs = draw_section_outputs(jax.random.fold_in(key_of[5], 71), 0)
    norm_gain = jnp.clip(1.0 + 0.18 * jax.random.normal(key_of[2], (SECTIONS, D), jnp.float32), 0.1, 1.9)
    input_grads = draw_input_grads(jax.random.fold_in(key_of[5], 71), 0)
    loss_grads = draw_loss_grads(jax.random.fold_in(key_of[5], 71), 0)
    return dict(embeddings=embeddings, section_outputs=section_outputs, norm_gain=norm_gain, input_grads=input_grads, loss_grads=loss_grads)


def normalize(hidden_rows, gain_row):
    values = hidden_rows.astype(jnp.float32)
    row_mean = lax.optimization_barrier(jnp.sum(values, axis=1, keepdims=True)) / D
    row_power = lax.optimization_barrier(jnp.sum(values * values, axis=1, keepdims=True)) / D
    scaled = (values - row_mean) * lax.rsqrt(row_power - row_mean * row_mean + 1e-05)
    return (scaled * gain_row).astype(jnp.bfloat16)

def factor_blocks(features):
    column_blocks = features.astype(jnp.float32).reshape(TOKENS, D // BLK, BLK)
    moments = jnp.einsum('tcb,tcd->cbd', column_blocks, column_blocks, precision=lax.Precision.HIGHEST) / TOKENS
    return moments + 0.05 * jnp.eye(BLK, dtype=jnp.float32)

def invert(damped):
    row_bound = lax.optimization_barrier(jnp.max(lax.optimization_barrier(jnp.sum(jnp.abs(damped), axis=2)), axis=1))[:, None, None]
    normed = damped / row_bound
    iterate = 2.0 * jnp.eye(BLK, dtype=jnp.float32) - normed
    for repeat in range(ITERS - 1):
        product = jnp.einsum('cij,cjk->cik', normed, iterate, precision=lax.Precision.HIGHEST)
        iterate = 2.0 * iterate - jnp.einsum('cij,cjk->cik', iterate, product, precision=lax.Precision.HIGHEST)
    return iterate / row_bound

def one_section(operands):
    hidden_rows, gain_row, grad_rows = operands
    inputs = normalize(hidden_rows, gain_row)
    return jnp.stack([invert(factor_blocks(inputs)), invert(factor_blocks(grad_rows))])

def reference(embeddings, section_outputs, norm_gain, input_grads, loss_grads):
    hidden_states = jnp.concatenate([embeddings[None], section_outputs[:-1]], axis=0)
    output_grads = jnp.concatenate([input_grads[1:], loss_grads[None]], axis=0)
    return lax.map(one_section, (hidden_states, norm_gain, output_grads))
```

```python
import functools

import jax
import jax.numpy as jnp
from jax import lax
from jax.experimental import pallas as pl
from jax.experimental.pallas import tpu as pltpu
from jax.sharding import PartitionSpec as P

D = 6144
BLK = 768
TOKENS = 2048
SECTIONS, REPLICAS, HALVES = 16, 8, 2
ROWS = TOKENS // REPLICAS
COLS = D // HALVES
AXES = ("section", "dp", "tensor")
ROUNDS = [(rx, rk) for rk in range(2) for rx in range(4)]


def device_index(s, d, h):
    return (s * REPLICAS + d) * HALVES + h


def route(rx, rk):
    pairs = []
    for s in range(SECTIONS):
        for d in range(REPLICAS):
            for h in range(HALVES):
                kind = (d // 4) ^ rk
                j = (d % 4 + rx) % 4
                to = (s + 1) % SECTIONS if kind == 0 else (s - 1) % SECTIONS
                pairs.append((device_index(s, d, h), device_index(to, 4 * h + j, kind)))
    return pairs


def chunk_kernel(emb, outs, grads, loss, *rest):
    chunks, sems = rest[:8], rest[8]
    s = lax.axis_index("section")
    d = lax.axis_index("dp")
    x, ylo = lax.rem(d, 4), lax.div(d, 4)

    def copies(r, src):
        rx, rk = ROUNDS[r]
        j = lax.rem(x + rx, 4)
        cols = pl.ds(pl.multiple_of(j * BLK, BLK), BLK)
        return pltpu.make_async_copy(src.at[:, cols], chunks[r], sems.at[r])

    for r, (rx, rk) in enumerate(ROUNDS):
        kind = lax.rem(ylo + rk, 2)
        edge = jnp.where(kind == 0, s == SECTIONS - 1, s == 0)
        for k, e, src in ((0, True, emb), (0, False, outs), (1, True, loss), (1, False, grads)):
            @pl.when((kind == k) & (edge == e))
            def _():
                copies(r, src).start()
    for r in range(8):
        copies(r, outs).wait()


def make_chunks(emb, outs, grads, loss):
    any_spec = pl.BlockSpec(memory_space=pl.ANY)
    return pl.pallas_call(
        chunk_kernel,
        out_shape=[jax.ShapeDtypeStruct((ROWS, BLK), jnp.bfloat16)] * 8,
        in_specs=[any_spec] * 4,
        out_specs=[any_spec] * 8,
        scratch_shapes=[pltpu.SemaphoreType.DMA((8,))],
        name="chunks",
    )(emb, outs, grads, loss)


def gram_kernel(acc, chunk, mean, scale, gain, out):
    rows = chunk[...].astype(jnp.float32)
    rows = ((rows - mean[...]) * scale[...] * gain[...]).astype(jnp.bfloat16)
    part = lax.dot_general(
        rows, rows, (((0,), (0,)), ((), ())), preferred_element_type=jnp.float32
    )
    if acc is None:
        out[...] = part
    else:
        out[...] = acc[...] + part


def gram(acc, chunk, mean, scale, gain):
    vmem = pl.BlockSpec(memory_space=pltpu.VMEM)
    args = [chunk, mean, scale, gain]
    body = functools.partial(gram_kernel, None)
    aliases = {}
    if acc is not None:
        args = [acc] + args
        body = gram_kernel
        aliases = {0: 0}
    return pl.pallas_call(
        body,
        out_shape=jax.ShapeDtypeStruct((BLK, BLK), jnp.float32),
        in_specs=[vmem] * len(args),
        out_specs=vmem,
        input_output_aliases=aliases,
        compiler_params=pltpu.CompilerParams(vmem_limit_bytes=32 * 2**20),
        name="gram",
    )(*args)


def split(a):
    hi = a.astype(jnp.bfloat16)
    return hi, (a - hi.astype(jnp.float32)).astype(jnp.bfloat16)


def times(a, b):
    def dot(p, q):
        return jnp.dot(p, q, preferred_element_type=jnp.float32)

    return dot(a[0], b[0]) + (dot(a[0], b[1]) + dot(a[1], b[0]))


def invert_kernel(total, out):
    row = lax.broadcasted_iota(jnp.int32, (BLK, BLK), 0)
    col = lax.broadcasted_iota(jnp.int32, (BLK, BLK), 1)
    eye = jnp.where(row == col, 1.0, 0.0).astype(jnp.float32)
    damped = total[...] * (1.0 / TOKENS) + 0.05 * eye
    bound = jnp.max(jnp.sum(jnp.abs(damped), axis=1, keepdims=True))
    first = eye - damped / bound
    first_parts = split(first)
    second = times(first_parts, first_parts)
    second_parts = split(second)
    low = eye + first + second + times(first_parts, second_parts)
    fourth = times(second_parts, second_parts)
    out[...] = (low + times(split(low), split(fourth))) / bound


def invert(total):
    vmem = pl.BlockSpec(memory_space=pltpu.VMEM)
    return pl.pallas_call(
        invert_kernel,
        out_shape=jax.ShapeDtypeStruct((BLK, BLK), jnp.float32),
        in_specs=[vmem],
        out_specs=vmem,
        compiler_params=pltpu.CompilerParams(vmem_limit_bytes=48 * 2**20),
        name="invert",
    )(total)


def per_device(embeddings, section_outputs, norm_gain, input_grads, loss_grads):
    s = lax.axis_index("section")
    d = lax.axis_index("dp")
    h = lax.axis_index("tensor")
    sent = section_outputs[0]
    chunks = make_chunks(embeddings, sent, input_grads[0], loss_grads)
    arrived = [lax.ppermute(c, AXES, route(*r)) for c, r in zip(chunks, ROUNDS)]

    other_gain = lax.ppermute(norm_gain, "tensor", [(0, 1), (1, 0)])
    gain_half = jnp.where(d // 4 == 0, norm_gain, other_gain)
    gain = lax.dynamic_slice(gain_half, (0, (d % 4) * BLK), (1, BLK))
    gain = jnp.where(h == 0, gain, 1.0)

    values = jnp.where(s == SECTIONS - 1, embeddings, sent).astype(jnp.float32)
    sums = jnp.stack([jnp.sum(values, axis=1), jnp.sum(values * values, axis=1)])
    gathered = lax.all_gather(sums, ("dp", "tensor"))
    stats = jnp.sum(gathered.reshape(REPLICAS, HALVES, 2, ROWS), axis=1)
    stats = lax.ppermute(stats, "section", [(i, (i + 1) % SECTIONS) for i in range(SECTIONS)])
    mean = stats[:, 0] / D
    power = stats[:, 1] / D
    scale = lax.rsqrt(power - mean * mean + 1e-05)
    mean = jnp.where(h == 0, mean, 0.0)[:, :, None]
    scale = jnp.where(h == 0, scale, 1.0)[:, :, None]

    total = None
    for chunk, (rx, rk) in zip(arrived, ROUNDS):
        source = (h ^ rk) * 4 + (d % 4 + 4 - rx) % 4
        total = gram(
            total,
            chunk,
            lax.dynamic_index_in_dim(mean, source, 0, False),
            lax.dynamic_index_in_dim(scale, source, 0, False),
            gain,
        )
    return invert(total).reshape(1, 1, 1, BLK, BLK)


def solution(mesh):
    placed = (
        P("dp", "tensor"),
        P("section", "dp", "tensor"),
        P("section", "tensor"),
        P("section", "dp", "tensor"),
        P("dp", "tensor"),
    )
    return jax.shard_map(
        per_device,
        mesh=mesh,
        in_specs=placed,
        out_specs=P("section", "tensor", "dp", None, None),
        check_vma=False,
    )
```

```python
import functools

import jax
import jax.numpy as jnp
from jax import lax
from jax.experimental import pallas as pl
from jax.experimental.pallas import tpu as pltpu
from jax.sharding import PartitionSpec as P

D = 6144
BLK = 768
TOKENS = 2048
SECTIONS, REPLICAS, HALVES = 16, 8, 2
ROWS = TOKENS // REPLICAS
COLS = D // HALVES
AXES = ("section", "dp", "tensor")


def pairs(move):
    out = []
    for s in range(SECTIONS):
        for d in range(REPLICAS):
            for h in range(HALVES):
                to_s, x, y = move(s, d % 4, 2 * h + d // 4)
                to = ((to_s % SECTIONS) * REPLICAS + (y % 2) * 4 + x % 4) * HALVES + y // 2
                out.append(((s * REPLICAS + d) * HALVES + h, to))
    return out


def across(shift, own):
    def move(s, x, y):
        kind = y // 2 if own else 1 - y // 2
        return (s + 1 if kind == 0 else s - 1), x + shift, y

    return pairs(move)


SIGMA = pairs(lambda s, x, y: (s, x, y ^ 3))
TAU = pairs(lambda s, x, y: (s, x, y ^ 1))


def send(block, route):
    return lax.ppermute(block, AXES, route)


CUTS = [(False, 2), (False, 1), (False, 3), (True, 1), (True, 3), (False, 0), (True, 2), (True, 0)]


def cut_kernel(emb, outs, grads, loss, *rest):
    chunks, sems = rest[:-1], rest[-1]
    s = lax.axis_index("section")
    x = lax.rem(lax.axis_index("dp"), 4)
    h = lax.axis_index("tensor")

    def copy(r, src):
        j = lax.rem(x + CUTS[r][1], 4)
        cols = pl.ds(pl.multiple_of(j * BLK, BLK), BLK)
        return pltpu.make_async_copy(src.at[:, cols], chunks[r], sems.at[r])

    for r, (own, _) in enumerate(CUTS):
        kind = h if own else 1 - h
        edge = jnp.where(kind == 0, s == SECTIONS - 1, s == 0)
        for k, e, src in ((0, True, emb), (0, False, outs), (1, True, loss), (1, False, grads)):
            @pl.when((kind == k) & (edge == e))
            def _():
                copy(r, src).start()
    for r in range(len(CUTS)):
        copy(r, outs).wait()


def cut(emb, outs, grads, loss):
    any_spec = pl.BlockSpec(memory_space=pl.ANY)
    vmem = pl.BlockSpec(memory_space=pltpu.VMEM)
    return pl.pallas_call(
        cut_kernel,
        out_shape=[jax.ShapeDtypeStruct((ROWS, BLK), jnp.bfloat16)] * len(CUTS),
        in_specs=[any_spec] * 4,
        out_specs=[vmem] * len(CUTS),
        scratch_shapes=[pltpu.SemaphoreType.DMA((len(CUTS),))],
        name="cut",
    )(emb, outs, grads, loss)


def normed(chunk, mean, scale, gain):
    return ((chunk.astype(jnp.float32) - mean) * scale * gain).astype(jnp.bfloat16)


def pair_gram(first, second, sums, gain_row):
    is_input = lax.axis_index("tensor") == 0
    mean = sums[:, 0] / D
    power = sums[:, 1] / D
    scale = lax.rsqrt(power - mean * mean + 1e-05)
    mean = jnp.where(is_input, mean, 0.0)
    scale = jnp.where(is_input, scale, 1.0)
    gain = jnp.where(is_input, gain_row, 1.0)
    cols = jnp.concatenate([mean, scale, mean, scale], axis=0).T
    rows = jnp.concatenate(
        [
            normed(first, cols[:, 0:1], cols[:, 2:3], gain),
            normed(second, cols[:, 1:2], cols[:, 3:4], gain),
        ],
        axis=0,
    )
    return lax.dot_general(
        rows, rows, (((0,), (0,)), ((), ())), preferred_element_type=jnp.float32
    )


def is_keeper():
    return lax.axis_index("tensor") == lax.div(lax.axis_index("dp"), 4)


def gram_kernel(gain, sums2, k2, t2, sums0, k0, t0, out):
    out[...] = pair_gram(k2[...], t2[...], sums2[...], gain[...])
    out[...] += pair_gram(k0[...], t0[...], sums0[...], gain[...])


def gram_more_kernel(acc, gain, sums, b, a, t, out):
    kept = jnp.where(is_keeper(), b[...], a[...])
    out[...] = acc[...] + pair_gram(kept, t[...], sums[...], gain[...])


def split(a):
    hi = a.astype(jnp.bfloat16)
    return hi, (a - hi.astype(jnp.float32)).astype(jnp.bfloat16)


def times(a, b):
    def dot(p, q):
        return jnp.dot(p, q, preferred_element_type=jnp.float32)

    return dot(a[0], b[0]) + (dot(a[0], b[1]) + dot(a[1], b[0]))


def invert(total):
    row = lax.broadcasted_iota(jnp.int32, (BLK, BLK), 0)
    col = lax.broadcasted_iota(jnp.int32, (BLK, BLK), 1)
    eye = jnp.where(row == col, 1.0, 0.0).astype(jnp.float32)
    damped = total * (1.0 / TOKENS) + 0.05 * eye
    bound = jnp.max(jnp.sum(jnp.abs(damped), axis=1, keepdims=True))
    first = eye - damped / bound
    first_parts = split(first)
    second = times(first_parts, first_parts)
    second_parts = split(second)
    low = eye + first + second + times(first_parts, second_parts)
    fourth = times(second_parts, second_parts)
    return (low + times(split(low), split(fourth))) / bound


def last_kernel(acc, gain, sums, b, a, t, out):
    kept = jnp.where(is_keeper(), b[...], a[...])
    out[...] = invert(acc[...] + pair_gram(kept, t[...], sums[...], gain[...]))


def in_vmem(kernel, name, *args):
    vmem = pl.BlockSpec(memory_space=pltpu.VMEM)
    return pl.pallas_call(
        kernel,
        out_shape=jax.ShapeDtypeStruct((BLK, BLK), jnp.float32),
        in_specs=[vmem] * len(args),
        out_specs=vmem,
        compiler_params=pltpu.CompilerParams(vmem_limit_bytes=48 * 2**20),
        name=name,
    )(*args)


def per_device(embeddings, section_outputs, norm_gain, input_grads, loss_grads):
    s = lax.axis_index("section")
    d = lax.axis_index("dp")
    h = lax.axis_index("tensor")
    keeper = h == d // 4
    sent = section_outputs[0]

    a2, a1, a3, b1, b3, a0, b2, b0 = cut(embeddings, sent, input_grads[0], loss_grads)

    ra2 = send(a2, SIGMA)
    xa1 = send(a1, across(1, False))
    xa3 = send(a3, across(3, False))
    xb1 = send(b1, across(1, True))
    xb3 = send(b3, across(3, True))

    values = jnp.where(s == SECTIONS - 1, embeddings, sent).astype(jnp.float32)
    sums = jnp.stack([jnp.sum(values, axis=1), jnp.sum(values * values, axis=1)])
    other = send(jnp.concatenate([sums.reshape(1, -1), norm_gain], axis=1), SIGMA)
    crossed = other[0, : 2 * ROWS].reshape(2, ROWS)
    gain_half = jnp.where(d // 4 == 0, norm_gain, other[:, 2 * ROWS :])
    gain = lax.dynamic_slice(gain_half, (0, (d % 4) * BLK), (1, BLK))
    beside = send(jnp.stack([crossed, sums]), TAU)
    full = jnp.stack([sums, crossed]) + beside
    full = jnp.where(keeper, full, full[::-1])
    stats = {i: send(full, across(i, True)) for i in range(4)}

    t2 = jnp.where(keeper, ra2, b2)
    k2 = jnp.where(keeper, b2, ra2)
    t2 = send(t2, TAU)
    ra0 = send(a0, SIGMA)
    t0 = jnp.where(keeper, ra0, b0)
    k0 = jnp.where(keeper, b0, ra0)
    t0 = send(t0, TAU)
    ra1 = send(xa1, SIGMA)
    xk2 = send(k2, across(2, True))
    xt2 = send(t2, across(2, True))
    ra3 = send(xa3, SIGMA)
    t1 = send(jnp.where(keeper, ra1, xb1), TAU)
    xk0 = send(k0, across(0, True))
    xt0 = send(t0, across(0, True))
    t3 = send(jnp.where(keeper, ra3, xb3), TAU)

    total = in_vmem(gram_kernel, "gram20", gain, stats[2], xk2, xt2, stats[0], xk0, xt0)
    total = in_vmem(gram_more_kernel, "gram1", total, gain, stats[1], xb1, ra1, t1)
    result = in_vmem(last_kernel, "gram3", total, gain, stats[3], xb3, ra3, t3)
    return result.reshape(1, 1, 1, BLK, BLK)


def solution(mesh):
    placed = (
        P("dp", "tensor"),
        P("section", "dp", "tensor"),
        P("section", "tensor"),
        P("section", "dp", "tensor"),
        P("dp", "tensor"),
    )
    return jax.shard_map(
        per_device,
        mesh=mesh,
        in_specs=placed,
        out_specs=P("section", "tensor", "dp", None, None),
        check_vma=False,
    )
```

```python
import functools

import jax
import jax.numpy as jnp
from jax import lax
from jax.experimental import pallas as pl
from jax.experimental.pallas import tpu as pltpu
from jax.sharding import PartitionSpec as P

D = 6144
BLK = 768
TOKENS = 2048
SECTIONS, REPLICAS, HALVES = 16, 8, 2
ROWS = TOKENS // REPLICAS
COLS = D // HALVES
EXTRA = 16
AXES = ("section", "dp", "tensor")


def pairs(move):
    out = []
    for s in range(SECTIONS):
        for d in range(REPLICAS):
            for h in range(HALVES):
                to_s, x, y = move(s, d % 4, 2 * h + d // 4)
                to = ((to_s % SECTIONS) * REPLICAS + (y % 2) * 4 + x % 4) * HALVES + y // 2
                out.append(((s * REPLICAS + d) * HALVES + h, to))
    return out


def across(shift, own):
    def move(s, x, y):
        kind = y // 2 if own else 1 - y // 2
        return (s + 1 if kind == 0 else s - 1), x + shift, y

    return pairs(move)


SIGMA = pairs(lambda s, x, y: (s, x, y ^ 3))
TAU = pairs(lambda s, x, y: (s, x, y ^ 1))


CUTS = [(own, shift) for own in (False, True) for shift in range(4)]


def send(name, block, route, *after):
    with jax.named_scope(name):
        if after:
            block = lax.optimization_barrier((block, *after))[0]
        return lax.ppermute(block, AXES, route)


def coded(rows):
    parts = []
    for _ in range(3):
        parts.append(rows.astype(jnp.bfloat16))
        rows = rows - parts[-1].astype(jnp.float32)
    return jnp.concatenate(parts, axis=1)


def decoded(block):
    block = block.astype(jnp.float32)
    return block[:, :ROWS] + block[:, ROWS : 2 * ROWS] + block[:, 2 * ROWS :]


PARTS = 4


def cut_kernel(emb, outs, grads, loss, *rest):
    chunks, (hidden, grad, tail, in_sems, out_sems, tail_sems) = rest[:-6], rest[-6:]
    s = lax.axis_index("section")
    x = lax.rem(lax.axis_index("dp"), 4)
    h = lax.axis_index("tensor")
    step = ROWS // PARTS

    def load(source, target, part, sem):
        rows = pl.ds(part * step, step)
        return pltpu.make_async_copy(source.at[rows], target.at[rows], in_sems.at[sem + part])

    for edge in (True, False):
        for section, source, target, sem in (
            (SECTIONS - 1, emb if edge else outs, hidden, 0),
            (0, loss if edge else grads, grad, PARTS),
        ):
            @pl.when((s == section) == edge)
            def _():
                for part in range(PARTS):
                    load(source, target, part, sem).start()

    for part in range(PARTS):
        load(outs, hidden, part, 0).wait()
    for part in range(PARTS):
        load(grads, grad, part, PARTS).wait()

    def store(r, source):
        cols = pl.ds(pl.multiple_of(lax.rem(x + CUTS[r][1], 4) * BLK, BLK), BLK)
        return pltpu.make_async_copy(source.at[:, cols], chunks[r].at[:ROWS], out_sems.at[r])

    for r, (own, _) in enumerate(CUTS):
        for kind, source in ((0, hidden), (1, grad)):
            @pl.when((h == kind) == own)
            def _():
                store(r, source).start()

    values = hidden[...].astype(jnp.float32)
    total = jnp.sum(values, axis=1, keepdims=True)
    power = jnp.sum(values * values, axis=1, keepdims=True)
    odd = lax.broadcasted_iota(jnp.int32, (ROWS, 128), 1) % 2 == 1
    tail[...] = coded(jnp.where(odd, power, total).T[:EXTRA, :])
    tails = [
        pltpu.make_async_copy(tail, chunk.at[ROWS:], tail_sems.at[r])
        for r, chunk in enumerate(chunks)
    ]
    for copy in tails:
        copy.start()
    for r in range(len(CUTS)):
        store(r, hidden).wait()
    for copy in tails:
        copy.wait()


def cut(emb, outs, grads, loss):
    any_spec = pl.BlockSpec(memory_space=pl.ANY)
    return pl.pallas_call(
        cut_kernel,
        out_shape=[jax.ShapeDtypeStruct((ROWS + EXTRA, BLK), jnp.bfloat16)] * len(CUTS),
        in_specs=[any_spec] * 4,
        out_specs=[any_spec] * len(CUTS),
        scratch_shapes=[
            pltpu.VMEM((ROWS, COLS), jnp.bfloat16),
            pltpu.VMEM((ROWS, COLS), jnp.bfloat16),
            pltpu.VMEM((EXTRA, BLK), jnp.bfloat16),
            pltpu.SemaphoreType.DMA((2 * PARTS,)),
            pltpu.SemaphoreType.DMA((len(CUTS),)),
            pltpu.SemaphoreType.DMA((len(CUTS),)),
        ],
        name="cut",
    )(emb, outs, grads, loss)


def relay_kernel(a, b, onward, *kept):
    keeper = keeps()
    onward[:ROWS, :] = jnp.where(keeper, a[:ROWS, :], b[:ROWS, :])
    crossed = lax.broadcasted_iota(jnp.int32, (EXTRA, BLK), 0) % 4 >= 2
    onward[ROWS:, :] = jnp.where(crossed, a[ROWS:, :], b[ROWS:, :])
    for out in kept:
        out[...] = jnp.where(keeper, b[:ROWS, :], a[:ROWS, :])


def relay(a, b, with_kept=False):
    vmem = pl.BlockSpec(memory_space=pltpu.VMEM)
    shapes = [jax.ShapeDtypeStruct((rows, BLK), jnp.bfloat16) for rows in (ROWS + EXTRA, ROWS)]
    shapes = shapes[: 1 + with_kept]
    return pl.pallas_call(
        relay_kernel,
        out_shape=shapes,
        in_specs=[vmem] * 2,
        out_specs=[vmem] * len(shapes),
        compiler_params=pltpu.CompilerParams(vmem_limit_bytes=4 * 2**20),
        name="relay",
    )(a, b)


def forward_kernel(t, own, out):
    out[:ROWS, :] = t[:ROWS, :]
    first = lax.broadcasted_iota(jnp.int32, (EXTRA, BLK), 0) < 4
    out[ROWS:, :] = jnp.where(first, t[ROWS:, :], own[ROWS:, :])


def forward(t, own):
    vmem = pl.BlockSpec(memory_space=pltpu.VMEM)
    return pl.pallas_call(
        forward_kernel,
        out_shape=jax.ShapeDtypeStruct(t.shape, t.dtype),
        in_specs=[vmem] * 2,
        out_specs=vmem,
        compiler_params=pltpu.CompilerParams(vmem_limit_bytes=4 * 2**20),
        name="forward",
    )(t, own)


def gain_columns(gain, other):
    d = lax.axis_index("dp")
    x, first_half = lax.rem(d, 4), lax.div(d, 4) == 0
    cols = pl.ds(pl.multiple_of(x * BLK, BLK), BLK)
    return jnp.where(first_half, gain[:, cols], other[:, cols])


def pair_rows(first, second, mine, crossed, beside, relayed, gain_row):
    is_input = lax.axis_index("tensor") == 0
    same, swapped = mine + relayed, crossed + beside
    stats = jnp.concatenate(
        [jnp.where(keeps(), same, swapped), jnp.where(keeps(), swapped, same)] * 2, axis=0
    ).T / D
    gain = jnp.where(is_input, gain_row, 1.0)
    rows = []
    for chunk, c in ((first, 0), (second, 2)):
        mean, power = stats[:, c : c + 1], stats[:, c + 1 : c + 2]
        scale = jnp.where(is_input, lax.rsqrt(power - mean * mean + 1e-05), 1.0)
        mean = jnp.where(is_input, mean, 0.0)
        rows.append(((chunk.astype(jnp.float32) - mean) * scale * gain).astype(jnp.bfloat16))
    return rows


def gram(rows):
    rows = jnp.concatenate(rows, axis=0)
    return lax.dot_general(
        rows, rows, (((0,), (0,)), ((), ())), preferred_element_type=jnp.float32
    )


def keeps():
    return lax.axis_index("tensor") == lax.div(lax.axis_index("dp"), 4)


def early_rows(b, a, t, row):
    mine, crossed, rest = (decoded(r[ROWS:, :]) for r in (b, a, t))
    kept = jnp.where(keeps(), b[:ROWS, :], a[:ROWS, :])
    return pair_rows(kept, t[:ROWS, :], mine[:2], crossed[:2], rest[:2], rest[2:4], row)


def late_rows(k, t, row):
    rest = decoded(t[ROWS:, :])
    return pair_rows(k[...], t[:ROWS, :], rest[4:6], rest[6:8], rest[:2], rest[2:4], row)


def early_kernel(gain, other, b1, a1, t1, k0, t0, out):
    row = gain_columns(gain, other)
    out[...] = gram(early_rows(b1, a1, t1, row) + late_rows(k0, t0, row))


def split(a):
    hi = a.astype(jnp.bfloat16)
    return hi, (a - hi.astype(jnp.float32)).astype(jnp.bfloat16)


TILE = 256
STRIPES = [(slice(0, j + TILE), slice(j, j + TILE)) for j in range(0, BLK, TILE)]


def product(a, b, rows, cols):
    def dot(p, q):
        return jnp.dot(p[rows, :], q[:, cols], preferred_element_type=jnp.float32)

    return dot(a[0], b[0]) + dot(a[0], b[1]) + dot(a[1], b[0])


def put_symmetric(parts, rows, cols, value):
    for ref, part in zip(parts, split(value)):
        ref[rows, cols] = part
    if cols.start:
        above = slice(0, cols.start)
        for ref, part in zip(parts, split(value[above, :].T)):
            ref[cols, above] = part


def invert(total, out, first, second, fourth, low_parts, low, whole, sems):
    row = lax.broadcasted_iota(jnp.int32, (BLK, BLK), 0)
    col = lax.broadcasted_iota(jnp.int32, (BLK, BLK), 1)
    eye = jnp.where(row == col, 1.0, 0.0).astype(jnp.float32)
    damped = total * (1.0 / TOKENS) + 0.05 * eye
    bound = jnp.max(jnp.sum(jnp.abs(damped), axis=0, keepdims=True))
    inverse_bound = 1.0 / bound
    error = eye - damped * inverse_bound
    first[0][...], first[1][...] = split(error)
    low[...] = eye + error
    for rows, cols in STRIPES:
        value = product(first, first, rows, cols)
        put_symmetric(second, rows, cols, value)
        low[rows, cols] += value
    for rows, cols in STRIPES:
        value = low[rows, cols] + product(first, second, rows, cols)
        low[rows, cols] = value
        put_symmetric(low_parts, rows, cols, value)
        put_symmetric(fourth, rows, cols, product(second, second, rows, cols))
    copies = []
    for rows, cols in reversed(STRIPES):
        value = (low[rows, cols] + product(low_parts, fourth, rows, cols)) * inverse_bound
        whole[rows, cols] = value
        if cols.start:
            whole[cols, : cols.start] = value[: cols.start, :].T
        copies.append(pltpu.make_async_copy(whole.at[cols], out.at[cols], sems.at[len(copies)]))
        copies[-1].start()
    for copy in copies:
        copy.wait()


def last_kernel(acc, gain, other, b3, a3, t3, k2, t2, out, *scratch):
    row = gain_columns(gain, other)
    total = acc[...] + gram(early_rows(b3, a3, t3, row) + late_rows(k2, t2, row))
    pairs_of = [scratch[i : i + 2] for i in range(0, 8, 2)]
    invert(total, out, *pairs_of, *scratch[8:])


def in_vmem(kernel, name, args, out_space=pltpu.VMEM, scratch=()):
    vmem = pl.BlockSpec(memory_space=pltpu.VMEM)
    return pl.pallas_call(
        kernel,
        out_shape=jax.ShapeDtypeStruct((BLK, BLK), jnp.float32),
        in_specs=[vmem] * len(args),
        out_specs=pl.BlockSpec(memory_space=out_space),
        scratch_shapes=scratch,
        compiler_params=pltpu.CompilerParams(vmem_limit_bytes=32 * 2**20),
        name=name,
    )(*args)


def per_device(embeddings, section_outputs, norm_gain, input_grads, loss_grads):
    a0, a1, a2, a3, b0, b1, b2, b3 = cut(embeddings, section_outputs[0], input_grads[0], loss_grads)
    ra2 = send("sigma2", a2, SIGMA)
    xa1 = send("xa1", a1, across(1, False))
    xa3 = send("xa3", a3, across(3, False))
    ra0 = send("sigma0", a0, SIGMA)
    xb1 = send("xb1", b1, across(1, True))

    t2, k2 = relay(ra2, b2, True)
    rt2 = send("tau2", t2, TAU)
    ra1 = send("sigma1", xa1, SIGMA, ra2)
    xb3 = send("xb3", b3, across(3, True), xa3)
    t0, k0 = relay(ra0, b0, True)
    rt0 = send("tau0", t0, TAU)
    xk2 = send("xk2", k2, across(2, True), xb1)
    ra3 = send("sigma3", xa3, SIGMA, ra0)
    other = send("gain", norm_gain, SIGMA, rt2)
    xk0 = send("xk0", k0, across(0, True), xb3)
    rt1 = send("tau1", *relay(ra1, xb1), TAU, rt2)
    xt0 = send("xt0", forward(rt0, t0), across(0, True))
    xt2 = send("xt2", forward(rt2, t2), across(2, True), xb3, xk2)
    rt3 = send("tau3", *relay(ra3, xb3), TAU, rt0, other, xk0)

    total = in_vmem(early_kernel, "early", (norm_gain, other, xb1, ra1, rt1, xk0, xt0))
    square = (BLK, BLK)
    result = in_vmem(
        last_kernel,
        "last",
        (total, norm_gain, other, xb3, ra3, rt3, xk2, xt2),
        pl.ANY,
        [pltpu.VMEM(square, jnp.bfloat16)] * 8
        + [pltpu.VMEM(square, jnp.float32)] * 2
        + [pltpu.SemaphoreType.DMA((len(STRIPES),))],
    )
    return result.reshape(1, 1, 1, BLK, BLK)


def solution(mesh):
    placed = (
        P("dp", "tensor"),
        P("section", "dp", "tensor"),
        P("section", "tensor"),
        P("section", "dp", "tensor"),
        P("dp", "tensor"),
    )
    return jax.shard_map(
        per_device,
        mesh=mesh,
        in_specs=placed,
        out_specs=P("section", "tensor", "dp", None, None),
        check_vma=False,
    )
```

```python
import functools

import jax
import jax.numpy as jnp
from jax import lax
from jax.experimental import pallas as pl
from jax.experimental.pallas import tpu as pltpu
from jax.sharding import PartitionSpec as P

D = 6144
BLK = 768
TOKENS = 2048
SECTIONS, REPLICAS, HALVES = 16, 8, 2
ROWS = TOKENS // REPLICAS
COLS = D // HALVES
EXTRA = 16
AXES = ("section", "dp", "tensor")
BESIDE = pl.CostEstimate(flops=2 * 10**10, transcendentals=0, bytes_accessed=2**20)


def pairs(move):
    out = []
    for s in range(SECTIONS):
        for d in range(REPLICAS):
            for h in range(HALVES):
                to_s, x, y = move(s, d % 4, 2 * h + d // 4)
                to = ((to_s % SECTIONS) * REPLICAS + (y % 2) * 4 + x % 4) * HALVES + y // 2
                out.append(((s * REPLICAS + d) * HALVES + h, to))
    return out


def across(shift, own):
    def move(s, x, y):
        kind = y // 2 if own else 1 - y // 2
        return (s + 1 if kind == 0 else s - 1), x + shift, y

    return pairs(move)


SIGMA = pairs(lambda s, x, y: (s, x, y ^ 3))
TAU = pairs(lambda s, x, y: (s, x, y ^ 1))


FIRST_CUTS = [(False, 2), (False, 1), (False, 3)]
SECOND_CUTS = [(False, 0), (True, 1), (True, 3), (True, 0), (True, 2)]


def send(name, block, route, *after):
    with jax.named_scope(name):
        if after:
            block = lax.optimization_barrier((block, *after))[0]
        return lax.ppermute(block, AXES, route)


def split_three(values):
    parts = []
    for _ in range(3):
        parts.append(values.astype(jnp.bfloat16))
        values = values - parts[-1].astype(jnp.float32)
    return parts


def coded(rows):
    return jnp.concatenate(split_three(rows), axis=1)


def decoded(block):
    block = block.astype(jnp.float32)
    return block[:, :ROWS] + block[:, ROWS : 2 * ROWS] + block[:, 2 * ROWS :]


PARTS = 4


def cut_chunks(cuts, sources, held, sems):
    emb, outs, grads, loss = sources
    s = lax.axis_index("section")
    x = lax.rem(lax.axis_index("dp"), 4)
    h = lax.axis_index("tensor")

    def load(r, source):
        cols = pl.ds(pl.multiple_of(lax.rem(x + cuts[r][1], 4) * BLK, BLK), BLK)
        return pltpu.make_async_copy(source.at[:, cols], held.at[r], sems.at[r])

    for r, (own, _) in enumerate(cuts):
        kind = h if own else 1 - h
        edge = jnp.where(kind == 0, s == SECTIONS - 1, s == 0)
        for k, e, source in ((0, True, emb), (0, False, outs), (1, True, loss), (1, False, grads)):
            @pl.when((kind == k) & (edge == e))
            def _():
                load(r, source).start()
    return lambda r: load(r, outs).wait()


def first_cut_kernel(*refs):
    sources, chunks, tail_out = refs[:4], refs[4:7], refs[7]
    held, hidden, tail, in_sems, hidden_sems, out_sems, tail_sems = refs[8:]
    step = ROWS // PARTS

    def load(source, part):
        rows = pl.ds(part * step, step)
        return pltpu.make_async_copy(source.at[rows], hidden.at[rows], hidden_sems.at[part])

    wait = cut_chunks(FIRST_CUTS, sources, held, in_sems)
    last = lax.axis_index("section") == SECTIONS - 1
    for edge, source in ((True, sources[0]), (False, sources[1])):
        @pl.when(last == edge)
        def _():
            for part in range(PARTS):
                load(source, part).start()
    stores = []
    for r, chunk in enumerate(chunks):
        wait(r)
        stores.append(pltpu.make_async_copy(held.at[r], chunk.at[:ROWS], out_sems.at[r]))
        stores[-1].start()
    sums = []
    for part in range(PARTS):
        load(sources[1], part).wait()
        values = hidden[part * step : (part + 1) * step, :].astype(jnp.float32)
        total = jnp.sum(values, axis=1, keepdims=True)
        power = jnp.sum(values * values, axis=1, keepdims=True)
        odd = lax.broadcasted_iota(jnp.int32, (step, 128), 1) % 2 == 1
        sums.append(jnp.where(odd, power, total))
    tail[...] = coded(jnp.concatenate(sums, axis=0).T[:EXTRA, :])
    for i, target in enumerate((chunks[1].at[ROWS:], chunks[2].at[ROWS:], tail_out)):
        stores.append(pltpu.make_async_copy(tail, target, tail_sems.at[i]))
        stores[-1].start()
    for copy in stores:
        copy.wait()


def second_cut_kernel(*refs):
    sources, tail, chunks = refs[:4], refs[4], refs[5:10]
    held, in_sems, out_sems, tail_sems = refs[10:]
    wait = cut_chunks(SECOND_CUTS, sources, held, in_sems)
    stores = []
    for r, chunk in enumerate(chunks[:-1]):
        stores.append(pltpu.make_async_copy(tail, chunk.at[ROWS:], tail_sems.at[r]))
        stores[-1].start()
    for r, chunk in enumerate(chunks):
        wait(r)
        stores.append(pltpu.make_async_copy(held.at[r], chunk.at[:ROWS], out_sems.at[r]))
        stores[-1].start()
    for copy in stores:
        copy.wait()


def cut(*sources):
    any_spec = pl.BlockSpec(memory_space=pl.ANY)
    plain = jax.ShapeDtypeStruct((ROWS, BLK), jnp.bfloat16)
    summed = jax.ShapeDtypeStruct((ROWS + EXTRA, BLK), jnp.bfloat16)
    tail = jax.ShapeDtypeStruct((EXTRA, BLK), jnp.bfloat16)
    dma = pltpu.SemaphoreType.DMA
    *first, sums = pl.pallas_call(
        first_cut_kernel,
        out_shape=[plain, summed, summed, tail],
        in_specs=[any_spec] * 4,
        out_specs=[any_spec] * 4,
        scratch_shapes=[
            pltpu.VMEM((3, ROWS, BLK), jnp.bfloat16),
            pltpu.VMEM((ROWS, COLS), jnp.bfloat16),
            pltpu.VMEM((EXTRA, BLK), jnp.bfloat16),
            *(dma((n,)) for n in (3, PARTS, 3, 3)),
        ],
        name="cut1",
    )(*sources)
    second = pl.pallas_call(
        second_cut_kernel,
        out_shape=[summed] * 4 + [plain],
        in_specs=[any_spec] * 4 + [pl.BlockSpec(memory_space=pltpu.VMEM)],
        out_specs=[any_spec] * 5,
        scratch_shapes=[
            pltpu.VMEM((5, ROWS, BLK), jnp.bfloat16),
            *(dma((n,)) for n in (5, 5, 4)),
        ],
        name="cut2",
    )(*sources, sums)
    return *first, *second


def relay_kernel(a, b, onward, *kept):
    keeper = keeps()
    onward[:ROWS, :] = jnp.where(keeper, a[:ROWS, :], b[:ROWS, :])
    if onward.shape[0] > ROWS:
        crossed = lax.broadcasted_iota(jnp.int32, (EXTRA, BLK), 0) % 4 >= 2
        onward[ROWS:, :] = jnp.where(crossed, a[ROWS:, :], b[ROWS:, :])
    for out in kept:
        out[...] = jnp.where(keeper, b[...], a[...])


def relay(a, b, with_kept=False):
    vmem = pl.BlockSpec(memory_space=pltpu.VMEM)
    shapes = [jax.ShapeDtypeStruct(a.shape, a.dtype)] * (1 + with_kept)
    return pl.pallas_call(
        relay_kernel,
        out_shape=shapes,
        in_specs=[vmem] * 2,
        out_specs=[vmem] * len(shapes),
        compiler_params=pltpu.CompilerParams(vmem_limit_bytes=4 * 2**20),
        cost_estimate=BESIDE,
        name="relay",
    )(a, b)


def bundle_kernel(a0, b0, t0, own, t2, out0, out2):
    first = lax.broadcasted_iota(jnp.int32, (EXTRA, BLK), 0) < 4
    sums = jnp.where(first, t0[ROWS:, :], own[ROWS:, :])
    out2[:ROWS, :] = t2[...]
    out2[ROWS:, :] = sums
    out0[:ROWS, :] = jnp.where(keeps(), b0[:ROWS, :], a0[:ROWS, :])
    out0[ROWS : 2 * ROWS, :] = t0[:ROWS, :]
    out0[2 * ROWS :, :] = sums


def bundle(a0, b0, t0, own, t2):
    vmem = pl.BlockSpec(memory_space=pltpu.VMEM)
    return pl.pallas_call(
        bundle_kernel,
        out_shape=[
            jax.ShapeDtypeStruct((rows + EXTRA, BLK), jnp.bfloat16) for rows in (2 * ROWS, ROWS)
        ],
        in_specs=[vmem] * 5,
        out_specs=[vmem] * 2,
        compiler_params=pltpu.CompilerParams(vmem_limit_bytes=6 * 2**20),
        cost_estimate=BESIDE,
        name="bundle",
    )(a0, b0, t0, own, t2)


GAIN_ROW = 8


def own_gain(gain):
    x = lax.rem(lax.axis_index("dp"), 4)
    return gain[:, pl.ds(pl.multiple_of(x * BLK, BLK), BLK)]


def mark_kernel(chunk, gain, out, tail, sems):
    del chunk
    load = pltpu.make_async_copy(out.at[ROWS:], tail, sems.at[0])
    load.start()
    load.wait()
    row = lax.broadcasted_iota(jnp.int32, (EXTRA, BLK), 0)
    values = tail[...].astype(jnp.float32)
    for i, part in enumerate(split_three(own_gain(gain))):
        values = jnp.where(row == GAIN_ROW + i, part.astype(jnp.float32), values)
    tail[...] = values.astype(jnp.bfloat16)
    store = pltpu.make_async_copy(tail, out.at[ROWS:], sems.at[1])
    store.start()
    store.wait()


def mark(chunk, gain):
    any_spec = pl.BlockSpec(memory_space=pl.ANY)
    return pl.pallas_call(
        mark_kernel,
        out_shape=jax.ShapeDtypeStruct(chunk.shape, chunk.dtype),
        in_specs=[any_spec, pl.BlockSpec(memory_space=pltpu.VMEM)],
        out_specs=any_spec,
        scratch_shapes=[
            pltpu.VMEM((EXTRA, BLK), jnp.bfloat16),
            pltpu.SemaphoreType.DMA((2,)),
        ],
        input_output_aliases={0: 0},
        compiler_params=pltpu.CompilerParams(vmem_limit_bytes=4 * 2**20),
        cost_estimate=BESIDE,
        name="mark",
    )(chunk, gain)


def gain_columns(gain, marked):
    parts = marked[ROWS:, :].astype(jnp.float32)[GAIN_ROW : GAIN_ROW + 3]
    crossed = parts[0:1] + parts[1:2] + parts[2:3]
    return jnp.where(lax.div(lax.axis_index("dp"), 4) == 0, own_gain(gain), crossed)


def pair_rows(first, second, mine, crossed, beside, relayed, gain_row):
    is_input = lax.axis_index("tensor") == 0
    same, swapped = mine + relayed, crossed + beside
    stats = jnp.concatenate(
        [jnp.where(keeps(), same, swapped), jnp.where(keeps(), swapped, same)] * 2, axis=0
    ).T / D
    gain = jnp.where(is_input, gain_row, 1.0)
    rows = []
    for chunk, c in ((first, 0), (second, 2)):
        mean, power = stats[:, c : c + 1], stats[:, c + 1 : c + 2]
        scale = jnp.where(is_input, lax.rsqrt(power - mean * mean + 1e-05), 1.0)
        mean = jnp.where(is_input, mean, 0.0)
        rows.append(((chunk.astype(jnp.float32) - mean) * scale * gain).astype(jnp.bfloat16))
    return rows


def gram(rows):
    rows = jnp.concatenate(rows, axis=0)
    return lax.dot_general(
        rows, rows, (((0,), (0,)), ((), ())), preferred_element_type=jnp.float32
    )


def keeps():
    return lax.axis_index("tensor") == lax.div(lax.axis_index("dp"), 4)


def early_rows(b, a, t, row):
    mine, crossed, rest = (decoded(r[ROWS:, :]) for r in (b, a, t))
    kept = jnp.where(keeps(), b[:ROWS, :], a[:ROWS, :])
    return pair_rows(kept, t[:ROWS, :], mine[:2], crossed[:2], rest[:2], rest[2:4], row)


def late_rows(k, t, row):
    rest = decoded(t[ROWS:, :])
    return pair_rows(k[...], t[:ROWS, :], rest[4:6], rest[6:8], rest[:2], rest[2:4], row)


def early_kernel(gain, b1, a1, t1, out):
    out[...] = gram(early_rows(b1, a1, t1, gain_columns(gain, a1)))


def middle_kernel(acc, gain, a1, k2, t2, out):
    out[...] = acc[...] + gram(late_rows(k2, t2, gain_columns(gain, a1)))


def split(a):
    hi = a.astype(jnp.bfloat16)
    return hi, (a - hi.astype(jnp.float32)).astype(jnp.bfloat16)


TILE = 256
STRIPES = [(slice(i, i + TILE), slice(0, i + TILE)) for i in range(0, BLK, TILE)]


def product(a, b, rows, cols):
    left = jnp.concatenate([a[0][rows, :], a[0][rows, :], a[1][rows, :]], axis=1)
    right = jnp.concatenate([b[0][:, cols], b[1][:, cols], b[0][:, cols]], axis=0)
    return jnp.dot(left, right, preferred_element_type=jnp.float32)


def put_symmetric(refs, rows, cols, value, parts):
    for ref, part in zip(refs, parts(value)):
        ref[rows, cols] = part
    if rows.start:
        before = slice(0, rows.start)
        for ref, part in zip(refs, parts(value[:, before].T)):
            ref[before, rows] = part


def invert(out, first, second, fourth, low_parts, low, whole, sems):
    row = lax.broadcasted_iota(jnp.int32, (BLK, BLK), 0)
    col = lax.broadcasted_iota(jnp.int32, (BLK, BLK), 1)
    eye = jnp.where(row == col, 1.0, 0.0).astype(jnp.float32)
    damped = whole[...] * (1.0 / TOKENS) + 0.05 * eye
    bound = jnp.max(jnp.sum(jnp.abs(damped), axis=0, keepdims=True))
    inverse_bound = 1.0 / bound
    error = eye - damped * inverse_bound
    first[0][...], first[1][...] = split(error)
    low[...] = eye + error
    for rows, cols in STRIPES:
        value = product(first, first, rows, cols)
        put_symmetric(second, rows, cols, value, split)
        low[rows, cols] += value
    for rows, cols in STRIPES:
        value = low[rows, cols] + product(first, second, rows, cols)
        low[rows, cols] = value
        put_symmetric(low_parts, rows, cols, value, split)
        put_symmetric(fourth, rows, cols, product(second, second, rows, cols), split)
    copies = []
    for rows, cols in reversed(STRIPES):
        value = (low[rows, cols] + product(low_parts, fourth, rows, cols)) * inverse_bound
        put_symmetric([whole], rows, cols, value, lambda block: [block])
        copies.append(pltpu.make_async_copy(whole.at[rows], out.at[rows], sems.at[len(copies)]))
        copies[-1].start()
    for copy in copies:
        copy.wait()


def last_kernel(acc, gain, a1, b3, a3, t3, both0, out, *scratch):
    row = gain_columns(gain, a1)
    both0 = both0.at[:ROWS], both0.at[ROWS:]
    whole = scratch[9]
    whole[...] = acc[...] + gram(late_rows(*both0, row))
    whole[...] += gram(early_rows(b3, a3, t3, row))
    pairs_of = [scratch[i : i + 2] for i in range(0, 8, 2)]
    invert(out, *pairs_of, *scratch[8:])


def in_vmem(kernel, name, args, out_space=pltpu.VMEM, scratch=()):
    vmem = pl.BlockSpec(memory_space=pltpu.VMEM)
    return pl.pallas_call(
        kernel,
        out_shape=jax.ShapeDtypeStruct((BLK, BLK), jnp.float32),
        in_specs=[vmem] * len(args),
        out_specs=pl.BlockSpec(memory_space=out_space),
        scratch_shapes=scratch,
        compiler_params=pltpu.CompilerParams(vmem_limit_bytes=26 * 2**20),
        cost_estimate=pl.CostEstimate(
            flops=3 * 10**10, transcendentals=0, bytes_accessed=64 * 2**20
        ),
        name=name,
    )(*args)


def per_device(embeddings, section_outputs, norm_gain, input_grads, loss_grads):
    a2, a1, a3, a0, b1, b3, b0, b2 = cut(
        embeddings, section_outputs[0], input_grads[0], loss_grads
    )
    ra2 = send("sigma2", a2, SIGMA)
    xa1 = send("xa1", a1, across(1, False))
    xa3 = send("xa3", a3, across(3, False))
    ra0 = send("sigma0", a0, SIGMA)

    t2, k2 = relay(ra2, b2, True)
    rt2 = send("tau2", t2, TAU)
    ra1 = send("sigma1", mark(xa1, norm_gain), SIGMA, t2)
    xb1 = send("xb1", b1, across(1, True), xa1, xa3, t2)
    xb3 = send("xb3", b3, across(3, True), xa3, t2)
    (t0,) = relay(*lax.optimization_barrier((ra0, b0, rt2))[:2])
    rt0 = send("tau0", t0, TAU)
    ra3 = send("sigma3", xa3, SIGMA, ra0)
    xk2 = send("xk2", k2, across(2, True), xb1, xb3)
    rt1 = send("tau1", *relay(*lax.optimization_barrier((ra1, xb1, xb3))[:2]), TAU)
    both0, rt2 = bundle(ra0, b0, rt0, t0, rt2)
    xt2 = send("xt2", rt2, across(2, True))
    rt3 = send("tau3", *relay(*lax.optimization_barrier((ra3, xb3, both0))[:2]), TAU)
    both0 = send("both0", both0, across(0, True))

    total = in_vmem(early_kernel, "early", (norm_gain, xb1, ra1, rt1))
    total = in_vmem(middle_kernel, "middle", (total, norm_gain, ra1, xk2, xt2))
    square = (BLK, BLK)
    result = in_vmem(
        last_kernel,
        "last",
        (total, norm_gain, ra1, xb3, ra3, rt3, both0),
        pl.ANY,
        [pltpu.VMEM(square, jnp.bfloat16)] * 8
        + [pltpu.VMEM(square, jnp.float32)] * 2
        + [pltpu.SemaphoreType.DMA((len(STRIPES),))],
    )
    return result.reshape(1, 1, 1, BLK, BLK)


def solution(mesh):
    placed = (
        P("dp", "tensor"),
        P("section", "dp", "tensor"),
        P("section", "tensor"),
        P("section", "dp", "tensor"),
        P("dp", "tensor"),
    )
    return jax.shard_map(
        per_device,
        mesh=mesh,
        in_specs=placed,
        out_specs=P("section", "tensor", "dp", None, None),
        check_vma=False,
    )
```

```python
import functools

import jax
import jax.numpy as jnp
from jax import lax
from jax.experimental import pallas as pl
from jax.experimental.pallas import tpu as pltpu
from jax.sharding import PartitionSpec as P

D = 6144
BLK = 768
TOKENS = 2048
SECTIONS, REPLICAS, HALVES = 16, 8, 2
ROWS = TOKENS // REPLICAS
COLS = D // HALVES
EXTRA = 16
AXES = ("section", "dp", "tensor")
BESIDE = pl.CostEstimate(flops=2 * 10**10, transcendentals=0, bytes_accessed=2**20)


def pairs(move):
    out = []
    for s in range(SECTIONS):
        for d in range(REPLICAS):
            for h in range(HALVES):
                to_s, x, y = move(s, d % 4, 2 * h + d // 4)
                to = ((to_s % SECTIONS) * REPLICAS + (y % 2) * 4 + x % 4) * HALVES + y // 2
                out.append(((s * REPLICAS + d) * HALVES + h, to))
    return out


def across(shift, own):
    def move(s, x, y):
        kind = y // 2 if own else 1 - y // 2
        return (s + 1 if kind == 0 else s - 1), x + shift, y

    return pairs(move)


SIGMA = pairs(lambda s, x, y: (s, x, y ^ 3))
TAU = pairs(lambda s, x, y: (s, x, y ^ 1))


FIRST_CUTS = [(False, 2), (False, 1), (False, 3)]
SECOND_CUTS = [(False, 0), (True, 1), (True, 3), (True, 0), (True, 2)]


def send(name, block, route, *after):
    with jax.named_scope(name):
        if after:
            block = lax.optimization_barrier((block, *after))[0]
        return lax.ppermute(block, AXES, route)


def split_three(values):
    parts = []
    for _ in range(3):
        parts.append(values.astype(jnp.bfloat16))
        values = values - parts[-1].astype(jnp.float32)
    return parts


def coded(rows):
    return jnp.concatenate(split_three(rows), axis=1)


def decoded(block):
    block = block.astype(jnp.float32)
    return block[:, :ROWS] + block[:, ROWS : 2 * ROWS] + block[:, 2 * ROWS :]


PARTS = 4


def cut_chunks(cuts, sources, held, sems):
    emb, outs, grads, loss = sources
    s = lax.axis_index("section")
    x = lax.rem(lax.axis_index("dp"), 4)
    h = lax.axis_index("tensor")

    def load(r, source):
        cols = pl.ds(pl.multiple_of(lax.rem(x + cuts[r][1], 4) * BLK, BLK), BLK)
        return pltpu.make_async_copy(source.at[:, cols], held.at[r], sems.at[r])

    for r, (own, _) in enumerate(cuts):
        kind = h if own else 1 - h
        edge = jnp.where(kind == 0, s == SECTIONS - 1, s == 0)
        for k, e, source in ((0, True, emb), (0, False, outs), (1, True, loss), (1, False, grads)):
            @pl.when((kind == k) & (edge == e))
            def _():
                load(r, source).start()
    return lambda r: load(r, outs).wait()


def first_cut_kernel(*refs):
    sources, chunks, tail_out = refs[:4], refs[4:7], refs[7]
    held, hidden, tail, in_sems, hidden_sems, out_sems, tail_sems = refs[8:]
    step = ROWS // PARTS

    def load(source, part):
        rows = pl.ds(part * step, step)
        return pltpu.make_async_copy(source.at[rows], hidden.at[rows], hidden_sems.at[part])

    last = lax.axis_index("section") == SECTIONS - 1
    for edge, source in ((True, sources[0]), (False, sources[1])):
        @pl.when(last == edge)
        def _():
            for part in range(PARTS):
                load(source, part).start()
    wait = cut_chunks(FIRST_CUTS, sources, held, in_sems)
    stores = []
    sums = []
    for part in range(PARTS):
        load(sources[1], part).wait()
        values = hidden[part * step : (part + 1) * step, :].astype(jnp.float32)
        total = jnp.sum(values, axis=1, keepdims=True)
        power = jnp.sum(values * values, axis=1, keepdims=True)
        odd = lax.broadcasted_iota(jnp.int32, (step, 128), 1) % 2 == 1
        sums.append(jnp.where(odd, power, total))
        if 1 <= part <= len(chunks):
            wait(part - 1)
            store = pltpu.make_async_copy(
                held.at[part - 1], chunks[part - 1].at[:ROWS], out_sems.at[part - 1]
            )
            store.start()
            stores.append(store)
    tail[...] = coded(jnp.concatenate(sums, axis=0).T[:EXTRA, :])
    for i, target in enumerate((chunks[1].at[ROWS:], chunks[2].at[ROWS:], tail_out)):
        stores.append(pltpu.make_async_copy(tail, target, tail_sems.at[i]))
        stores[-1].start()
    for copy in stores:
        copy.wait()


def second_cut_kernel(*refs):
    sources, tail, chunks = refs[:4], refs[4], refs[5:10]
    held, in_sems, out_sems, tail_sems = refs[10:]
    wait = cut_chunks(SECOND_CUTS, sources, held, in_sems)
    stores = []
    for r, chunk in enumerate(chunks[:-1]):
        stores.append(pltpu.make_async_copy(tail, chunk.at[ROWS:], tail_sems.at[r]))
        stores[-1].start()
    for r, chunk in enumerate(chunks):
        wait(r)
        stores.append(pltpu.make_async_copy(held.at[r], chunk.at[:ROWS], out_sems.at[r]))
        stores[-1].start()
    for copy in stores:
        copy.wait()


def cut(*sources):
    any_spec = pl.BlockSpec(memory_space=pl.ANY)
    plain = jax.ShapeDtypeStruct((ROWS, BLK), jnp.bfloat16)
    summed = jax.ShapeDtypeStruct((ROWS + EXTRA, BLK), jnp.bfloat16)
    tail = jax.ShapeDtypeStruct((EXTRA, BLK), jnp.bfloat16)
    dma = pltpu.SemaphoreType.DMA
    *first, sums = pl.pallas_call(
        first_cut_kernel,
        out_shape=[plain, summed, summed, tail],
        in_specs=[any_spec] * 4,
        out_specs=[any_spec] * 4,
        scratch_shapes=[
            pltpu.VMEM((3, ROWS, BLK), jnp.bfloat16),
            pltpu.VMEM((ROWS, COLS), jnp.bfloat16),
            pltpu.VMEM((EXTRA, BLK), jnp.bfloat16),
            *(dma((n,)) for n in (3, PARTS, 3, 3)),
        ],
        name="cut1",
    )(*sources)
    second = pl.pallas_call(
        second_cut_kernel,
        out_shape=[summed] * 4 + [plain],
        in_specs=[any_spec] * 4 + [pl.BlockSpec(memory_space=pltpu.VMEM)],
        out_specs=[any_spec] * 5,
        scratch_shapes=[
            pltpu.VMEM((5, ROWS, BLK), jnp.bfloat16),
            *(dma((n,)) for n in (5, 5, 4)),
        ],
        name="cut2",
    )(*sources, sums)
    return *first, *second


def relay_kernel(a, b, onward, *kept):
    keeper = keeps()
    onward[:ROWS, :] = jnp.where(keeper, a[:ROWS, :], b[:ROWS, :])
    if onward.shape[0] > ROWS:
        crossed = lax.broadcasted_iota(jnp.int32, (EXTRA, BLK), 0) % 4 >= 2
        onward[ROWS:, :] = jnp.where(crossed, a[ROWS:, :], b[ROWS:, :])
    for out in kept:
        out[...] = jnp.where(keeper, b[...], a[...])


def relay(a, b, with_kept=False):
    vmem = pl.BlockSpec(memory_space=pltpu.VMEM)
    shapes = [jax.ShapeDtypeStruct(a.shape, a.dtype)] * (1 + with_kept)
    return pl.pallas_call(
        relay_kernel,
        out_shape=shapes,
        in_specs=[vmem] * 2,
        out_specs=[vmem] * len(shapes),
        compiler_params=pltpu.CompilerParams(vmem_limit_bytes=4 * 2**20),
        cost_estimate=BESIDE,
        name="relay",
    )(a, b)


def bundle_kernel(a0, b0, t0, own, t2, out0, out2):
    first = lax.broadcasted_iota(jnp.int32, (EXTRA, BLK), 0) < 4
    sums = jnp.where(first, t0[ROWS:, :], own[ROWS:, :])
    out2[:ROWS, :] = t2[...]
    out2[ROWS:, :] = sums
    out0[:ROWS, :] = jnp.where(keeps(), b0[:ROWS, :], a0[:ROWS, :])
    out0[ROWS : 2 * ROWS, :] = t0[:ROWS, :]
    out0[2 * ROWS :, :] = sums


def bundle(a0, b0, t0, own, t2):
    vmem = pl.BlockSpec(memory_space=pltpu.VMEM)
    return pl.pallas_call(
        bundle_kernel,
        out_shape=[
            jax.ShapeDtypeStruct((rows + EXTRA, BLK), jnp.bfloat16) for rows in (2 * ROWS, ROWS)
        ],
        in_specs=[vmem] * 5,
        out_specs=[vmem] * 2,
        compiler_params=pltpu.CompilerParams(vmem_limit_bytes=6 * 2**20),
        cost_estimate=BESIDE,
        name="bundle",
    )(a0, b0, t0, own, t2)


GAIN_ROW = 8


def own_gain(gain):
    x = lax.rem(lax.axis_index("dp"), 4)
    return gain[:, pl.ds(pl.multiple_of(x * BLK, BLK), BLK)]


def mark_kernel(chunk, gain, out, tail, sems):
    del chunk
    load = pltpu.make_async_copy(out.at[ROWS:], tail, sems.at[0])
    load.start()
    load.wait()
    row = lax.broadcasted_iota(jnp.int32, (EXTRA, BLK), 0)
    values = tail[...].astype(jnp.float32)
    for i, part in enumerate(split_three(own_gain(gain))):
        values = jnp.where(row == GAIN_ROW + i, part.astype(jnp.float32), values)
    tail[...] = values.astype(jnp.bfloat16)
    store = pltpu.make_async_copy(tail, out.at[ROWS:], sems.at[1])
    store.start()
    store.wait()


def mark(chunk, gain):
    any_spec = pl.BlockSpec(memory_space=pl.ANY)
    return pl.pallas_call(
        mark_kernel,
        out_shape=jax.ShapeDtypeStruct(chunk.shape, chunk.dtype),
        in_specs=[any_spec, pl.BlockSpec(memory_space=pltpu.VMEM)],
        out_specs=any_spec,
        scratch_shapes=[
            pltpu.VMEM((EXTRA, BLK), jnp.bfloat16),
            pltpu.SemaphoreType.DMA((2,)),
        ],
        input_output_aliases={0: 0},
        compiler_params=pltpu.CompilerParams(vmem_limit_bytes=4 * 2**20),
        cost_estimate=BESIDE,
        name="mark",
    )(chunk, gain)


def gain_columns(gain, marked):
    parts = marked[ROWS:, :].astype(jnp.float32)[GAIN_ROW : GAIN_ROW + 3]
    crossed = parts[0:1] + parts[1:2] + parts[2:3]
    return jnp.where(lax.div(lax.axis_index("dp"), 4) == 0, own_gain(gain), crossed)


def pair_rows(first, second, mine, crossed, beside, relayed, gain_row):
    is_input = lax.axis_index("tensor") == 0
    same, swapped = mine + relayed, crossed + beside
    stats = jnp.concatenate(
        [jnp.where(keeps(), same, swapped), jnp.where(keeps(), swapped, same)] * 2, axis=0
    ).T / D
    gain = jnp.where(is_input, gain_row, 1.0)
    rows = []
    for chunk, c in ((first, 0), (second, 2)):
        mean, power = stats[:, c : c + 1], stats[:, c + 1 : c + 2]
        scale = jnp.where(is_input, lax.rsqrt(power - mean * mean + 1e-05), 1.0)
        mean = jnp.where(is_input, mean, 0.0)
        rows.append(((chunk.astype(jnp.float32) - mean) * scale * gain).astype(jnp.bfloat16))
    return rows


def gram(rows):
    rows = jnp.concatenate(rows, axis=0)
    return lax.dot_general(
        rows, rows, (((0,), (0,)), ((), ())), preferred_element_type=jnp.float32
    )


def keeps():
    return lax.axis_index("tensor") == lax.div(lax.axis_index("dp"), 4)


def early_rows(b, a, t, row):
    mine, crossed, rest = (decoded(r[ROWS:, :]) for r in (b, a, t))
    kept = jnp.where(keeps(), b[:ROWS, :], a[:ROWS, :])
    return pair_rows(kept, t[:ROWS, :], mine[:2], crossed[:2], rest[:2], rest[2:4], row)


def late_rows(k, t, row):
    rest = decoded(t[ROWS:, :])
    return pair_rows(k[...], t[:ROWS, :], rest[4:6], rest[6:8], rest[:2], rest[2:4], row)


def early_kernel(gain, b1, a1, t1, out):
    out[...] = gram(early_rows(b1, a1, t1, gain_columns(gain, a1)))


def middle_kernel(acc, gain, a1, k2, t2, out):
    out[...] = acc[...] + gram(late_rows(k2, t2, gain_columns(gain, a1)))


def split(a):
    hi = a.astype(jnp.bfloat16)
    return hi, (a - hi.astype(jnp.float32)).astype(jnp.bfloat16)


TILE, LANES = 256, 128
STRIPES = [(slice(i, i + TILE), slice(0, i + TILE)) for i in range(0, BLK, TILE)]


def product(a, b, rows, cols):
    left = jnp.concatenate([a[0][rows, :], a[0][rows, :], a[1][rows, :]], axis=1)
    right = jnp.concatenate([b[0][:, cols], b[1][:, cols], b[0][:, cols]], axis=0)
    return jnp.dot(left, right, preferred_element_type=jnp.float32)


def put_symmetric(refs, rows, cols, value, parts):
    for ref, part in zip(refs, parts(value)):
        ref[rows, cols] = part
    if rows.start:
        before = slice(0, rows.start)
        for ref, part in zip(refs, parts(value[:, before].T)):
            ref[before, rows] = part


def invert(out, first, second, fourth, low_parts, low, whole, sems):
    bound = jnp.max(jnp.sum(jnp.abs(whole[...]), axis=0, keepdims=True)) * (1.0 / TOKENS) + 0.05
    inverse_bound = 1.0 / bound
    row = lax.broadcasted_iota(jnp.int32, (LANES, LANES), 0)
    col = lax.broadcasted_iota(jnp.int32, (LANES, LANES), 1)
    eye = jnp.where(row == col, 1.0, 0.0).astype(jnp.float32)
    for start in range(0, BLK, LANES):
        end = start + LANES

        def add_to_diagonal(block, amount):
            pieces = [block[:, :start], block[:, start:end] + amount * eye, block[:, end:]]
            return jnp.concatenate([piece for piece in pieces if piece.shape[1]], axis=1)

        error = whole[start:end, :] * (inverse_bound * (-1.0 / TOKENS))
        error = add_to_diagonal(error, 1.0 - 0.05 * inverse_bound)
        first[0][start:end, :], first[1][start:end, :] = split(error)
        low[start:end, :] = add_to_diagonal(error, 1.0)
    for rows, cols in STRIPES:
        value = product(first, first, rows, cols)
        put_symmetric(second, rows, cols, value, split)
        low[rows, cols] += value
    for rows, cols in STRIPES:
        value = low[rows, cols] + product(first, second, rows, cols)
        low[rows, cols] = value
        put_symmetric(low_parts, rows, cols, value, split)
        put_symmetric(fourth, rows, cols, product(second, second, rows, cols), split)
    copies = []
    for rows, cols in reversed(STRIPES):
        value = (low[rows, cols] + product(low_parts, fourth, rows, cols)) * inverse_bound
        put_symmetric([whole], rows, cols, value, lambda block: [block])
        copies.append(pltpu.make_async_copy(whole.at[rows], out.at[rows], sems.at[len(copies)]))
        copies[-1].start()
    for copy in copies:
        copy.wait()


def last_kernel(acc, gain, a1, b3, a3, t3, both0, out, *scratch):
    row = gain_columns(gain, a1)
    both0 = both0.at[:ROWS], both0.at[ROWS:]
    whole = scratch[9]
    whole[...] = acc[...] + gram(late_rows(*both0, row))
    whole[...] += gram(early_rows(b3, a3, t3, row))
    pairs_of = [scratch[i : i + 2] for i in range(0, 8, 2)]
    invert(out, *pairs_of, *scratch[8:])


def in_vmem(kernel, name, args, out_space=pltpu.VMEM, scratch=()):
    vmem = pl.BlockSpec(memory_space=pltpu.VMEM)
    return pl.pallas_call(
        kernel,
        out_shape=jax.ShapeDtypeStruct((BLK, BLK), jnp.float32),
        in_specs=[vmem] * len(args),
        out_specs=pl.BlockSpec(memory_space=out_space),
        scratch_shapes=scratch,
        compiler_params=pltpu.CompilerParams(vmem_limit_bytes=26 * 2**20),
        cost_estimate=pl.CostEstimate(
            flops=3 * 10**10, transcendentals=0, bytes_accessed=64 * 2**20
        ),
        name=name,
    )(*args)


def per_device(embeddings, section_outputs, norm_gain, input_grads, loss_grads):
    a2, a1, a3, a0, b1, b3, b0, b2 = cut(
        embeddings, section_outputs[0], input_grads[0], loss_grads
    )
    ra2 = send("sigma2", a2, SIGMA)
    xa1 = send("xa1", a1, across(1, False))
    xa3 = send("xa3", a3, across(3, False))
    ra0 = send("sigma0", a0, SIGMA)

    t2, k2 = relay(ra2, b2, True)
    rt2 = send("tau2", t2, TAU)
    ra1 = send("sigma1", mark(xa1, norm_gain), SIGMA, t2)
    xb1 = send("xb1", b1, across(1, True), xa1, xa3, t2)
    xb3 = send("xb3", b3, across(3, True), xa3, t2)
    (t0,) = relay(*lax.optimization_barrier((ra0, b0, rt2))[:2])
    rt0 = send("tau0", t0, TAU)
    ra3 = send("sigma3", xa3, SIGMA, ra0)
    xk2 = send("xk2", k2, across(2, True), xb1, xb3)
    rt1 = send("tau1", *relay(*lax.optimization_barrier((ra1, xb1, xb3))[:2]), TAU)
    both0, rt2 = bundle(ra0, b0, rt0, t0, rt2)
    xt2 = send("xt2", rt2, across(2, True))
    rt3 = send("tau3", *relay(*lax.optimization_barrier((ra3, xb3, both0))[:2]), TAU)
    both0 = send("both0", both0, across(0, True))

    total = in_vmem(early_kernel, "early", (norm_gain, xb1, ra1, rt1))
    total = in_vmem(middle_kernel, "middle", (total, norm_gain, ra1, xk2, xt2))
    square = (BLK, BLK)
    result = in_vmem(
        last_kernel,
        "last",
        (total, norm_gain, ra1, xb3, ra3, rt3, both0),
        pl.ANY,
        [pltpu.VMEM(square, jnp.bfloat16)] * 8
        + [pltpu.VMEM(square, jnp.float32)] * 2
        + [pltpu.SemaphoreType.DMA((len(STRIPES),))],
    )
    return result.reshape(1, 1, 1, BLK, BLK)


def solution(mesh):
    placed = (
        P("dp", "tensor"),
        P("section", "dp", "tensor"),
        P("section", "tensor"),
        P("section", "dp", "tensor"),
        P("dp", "tensor"),
    )
    return jax.shard_map(
        per_device,
        mesh=mesh,
        in_specs=placed,
        out_specs=P("section", "tensor", "dp", None, None),
        check_vma=False,
    )
```
